32 devices in a mesh: gy: 8 (over y, x, core), gz: 4 (over z).
Axes of the slice: x: 2, y: 2, z: 4, core: 2. Of those that a mesh axis runs over, the one named last changes fastest.
Arguments:
- volume: bfloat16 [64, 32, 16, 256], P(None, 'gy', 'gz'), may hold values from -2500 to 2500
- down_weight: bfloat16 [128, 64, 2, 2, 2], replicated, may hold values from -0.25 to 0.25
- conv_one: bfloat16 [3, 3, 128, 384], replicated, may hold values from -0.109375 to 0.109375
- conv_two: bfloat16 [3, 3, 128, 384], replicated, may hold values from -0.109375 to 0.109375
- norm_gain: float32 [3, 128], replicated, may hold values from 0.1 to 1.9
- norm_shift: float32 [3, 128], replicated, may hold values from -2.5 to 2.5
Outputs:
- features: bfloat16 [128, 16, 8, 128], P(None, 'gy', 'gz')
The draws below stay inside these ranges and needn't reach their ends.
All inputs are finite; a program needn't handle non-finite values.
Results may differ from the reference program's by a relative error of at most 0.0065.
Values may be sent and summed in bfloat16 or wider, within the bound.
A program may use at most 64 MiB of HBM per device.

```python
import math
from functools import partial
import jax
import jax.numpy as jnp
from jax import lax

CI = 64
CO = 128
YD = 2
YQ = 32
ZQ = 16
XQ = 256
N_GY = 8


def draw_volume(key, part):
    key_noise = jax.random.fold_in(key, 11)
    key_scale = jax.random.fold_in(key, 12)
    key_region = jax.random.fold_in(key, 13)
    key_offset = jax.random.fold_in(key, 14)
    key_channel = jax.random.fold_in(key, 15)
    key_base = jax.random.fold_in(key, 16)
    row_ramp = jnp.arange(YQ, dtype=jnp.float32) / (YQ - 1)
    depth_ramp = jnp.arange(ZQ, dtype=jnp.float32) / (ZQ - 1)
    row_region = jnp.arange(YQ, dtype=jnp.int32) * 4 // YQ
    depth_region = jnp.arange(ZQ, dtype=jnp.int32) * 4 // ZQ
    rough = jnp.exp(jax.random.uniform(key_scale, (YQ, ZQ, XQ), jnp.float32, 0.0, math.log(3.0)))
    region_gain = jnp.exp(jax.random.uniform(key_region, (4, 4), jnp.float32, 0.0, math.log(3.0)))
    region_field = region_gain[row_region][:, depth_region]
    offsets = jax.random.uniform(key_offset, (CI, 4, 4), jnp.float32, -2.0, 2.0)
    offset_field = offsets[:, row_region][:, :, depth_region]
    channel = jnp.exp(jax.random.uniform(key_channel, (CI,), jnp.float32, -0.4, 0.4))
    log_base = jax.random.uniform(key_base, (), jnp.float32, math.log(2.0), math.log(3.0))
    noise = jnp.clip(jax.random.normal(key_noise, (CI, YQ, ZQ, XQ), jnp.float32), -4.0, 4.0)
    ramp = jnp.exp(log_base * (row_ramp[:, None] + depth_ramp[None, :]))
    spatial = rough * (region_field * ramp)[:, :, None]
    values = (noise + offset_field[:, :, :, None]) * spatial[None] * channel[:, None, None, None]
    return values.astype(jnp.bfloat16)


def normal_values(key, shape, scale, reach, kind=jnp.bfloat16):
    array = scale * jax.random.normal(key, shape, jnp.float32)
    return jnp.clip(array, min=-reach, max=reach).astype(kind)


def setup_inputs(seed: int = 0) -> dict:
    seeds = jax.random.split(jax.random.key(seed), 7)
    return {
        "volume": draw_volume(jax.random.fold_in(seeds[6], 71), 0),
        "down_weight": normal_values(seeds[1], (CO, CI, 2, 2, 2), (CI * 8) ** -0.5, 0.25),
        "conv_one": normal_values(seeds[2], (3, 3, CO, 3 * CO), (27 * CO) ** -0.5, 0.109375),
        "conv_two": normal_values(seeds[3], (3, 3, CO, 3 * CO), (27 * CO) ** -0.5, 0.109375),
        "norm_gain": jnp.clip(1.0 + 0.18 * jax.random.normal(seeds[4], (3, CO), jnp.float32), 0.1, 1.9),
        "norm_shift": normal_values(seeds[5], (3, CO), 0.5, 2.5, jnp.float32),
    }


def leaky(value):
    return jnp.where(value >= 0.0, value, 0.01 * value)

def normalize(value, gain, shift):
    mean = lax.optimization_barrier(jnp.mean(value, axis=(1, 2, 3), keepdims=True))
    spread = lax.optimization_barrier(jnp.mean(jnp.square(value - mean), axis=(1, 2, 3), keepdims=True))
    scaled = (value - mean) / jnp.sqrt(spread + 1e-05)
    return leaky(scaled * gain[:, None, None, None] + shift[:, None, None, None])

def strided_block(volume, down_weight, index):
    start = (index * (2 * YD)).astype(jnp.int32)
    rows_in = lax.dynamic_slice_in_dim(volume, start, 2 * YD, 1).astype(jnp.float32)
    blocks = rows_in.reshape(CI, YD, 2, ZQ // 2, 2, XQ // 2, 2)
    return jnp.einsum('oiabc,iyazbxc->oyzx', down_weight.astype(jnp.float32), blocks, precision=lax.Precision.HIGHEST)

def convolve(field, conv_weight):
    kernel = conv_weight.astype(jnp.float32).reshape(3, 3, CO, 3, CO)
    kernel = jnp.transpose(kernel, (2, 4, 0, 1, 3))
    result = lax.conv_general_dilated(field.astype(jnp.float32)[None], kernel, (1, 1, 1), ((1, 1), (1, 1), (1, 1)), dimension_numbers=('NCDHW', 'OIDHW', 'NCDHW'), precision=lax.Precision.HIGHEST)
    return result[0]

def reference(volume, down_weight, conv_one, conv_two, norm_gain, norm_shift):
    coarse = lax.map(partial(strided_block, volume, down_weight), jnp.arange(N_GY, dtype=jnp.int32))
    coarse = jnp.moveaxis(coarse, 0, 1).reshape(CO, YD * N_GY, ZQ // 2, XQ // 2)
    first = normalize(coarse, norm_gain[0], norm_shift[0]).astype(jnp.bfloat16)
    second = normalize(convolve(first, conv_one), norm_gain[1], norm_shift[1]).astype(jnp.bfloat16)
    return normalize(convolve(second, conv_two), norm_gain[2], norm_shift[2]).astype(jnp.bfloat16)
```

```python
import functools

import jax
import jax.numpy as jnp
from jax import lax
from jax.experimental import pallas as pl
from jax.experimental.pallas import tpu as pltpu
from jax.sharding import PartitionSpec as P

MESH = pl.DeviceIdType.MESH
SIDES = [(dy, dz) for dy in (-1, 0, 1) for dz in (-1, 0, 1) if (dy, dz) != (0, 0)]


def strided(volume, down_weight):
    blocks = volume.reshape(
        volume.shape[0], volume.shape[1] // 2, 2, volume.shape[2] // 2, 2, volume.shape[3] // 2, 2
    )
    return jnp.einsum(
        "oiabc,iyazbxc->yzxo", down_weight, blocks, preferred_element_type=jnp.float32
    )


def kernel(
    ny, nz,
    coarse_ref, one_hbm, two_hbm, gain_ref, shift_ref, out_ref,
    one_ref, two_ref, stat_out, stat_in, rim_out, rim_in, field,
    load_sem, stat_send, stat_recv, rim_send, rim_recv,
):
    count = ny * nz
    my, mz = lax.axis_index("gy"), lax.axis_index("gz")
    me = my * nz + mz
    rows, depth, length, channels = coarse_ref.shape
    cells = rows * depth * length

    loads = [
        pltpu.make_async_copy(one_hbm, one_ref, load_sem.at[0]),
        pltpu.make_async_copy(two_hbm, two_ref, load_sem.at[1]),
    ]
    for load in loads:
        load.start()

    def device(k):
        flat = lax.rem(me + k, count)
        return (flat // nz, lax.rem(flat, nz))

    barrier = pltpu.get_barrier_semaphore()

    def greet(k, _):
        pl.semaphore_signal(barrier, inc=1, device_id=device(k), device_id_type=MESH)
        return 0

    lax.fori_loop(1, count, greet, 0)
    pl.semaphore_wait(barrier, count - 1)

    def present(side):
        y, z = my + side[0], mz + side[1]
        return (y >= 0) & (y < ny) & (z >= 0) & (z < nz)

    def outer(d, n):
        return {-1: slice(0, 1), 0: slice(1, n + 1), 1: slice(n + 1, n + 2)}[d]

    def inner(d, n):
        return {-1: slice(0, 1), 0: slice(0, n), 1: slice(n - 1, n)}[d]

    def rim_copy(turn, s):
        dy, dz = SIDES[s]
        opposite = len(SIDES) - 1 - s
        return pltpu.make_async_remote_copy(
            src_ref=rim_out.at[turn, inner(dy, rows), inner(dz, depth)],
            dst_ref=rim_in.at[turn, outer(-dy, rows), outer(-dz, depth)],
            send_sem=rim_send.at[turn, s],
            recv_sem=rim_recv.at[turn, opposite],
            device_id=(my + dy, mz + dz),
            device_id_type=MESH,
        )

    def rim_arrival(turn, s):
        dy, dz = SIDES[s]
        slot = rim_in.at[turn, outer(dy, rows), outer(dz, depth)]
        return pltpu.make_async_remote_copy(
            src_ref=slot, dst_ref=slot,
            send_sem=rim_send.at[turn, s], recv_sem=rim_recv.at[turn, s],
            device_id=(my, mz), device_id_type=MESH,
        )

    def stat_all(turn):
        block = stat_in.at[turn, pl.ds(0, count - 1)]
        return pltpu.make_async_remote_copy(
            src_ref=block, dst_ref=block,
            send_sem=stat_send.at[turn], recv_sem=stat_recv.at[turn],
            device_id=(my, mz), device_id_type=MESH,
        )

    def send(turn, value):
        mean = jnp.sum(value, axis=0, keepdims=True) / cells
        centred = value - mean
        spread = jnp.sum(centred * centred, axis=0, keepdims=True)
        stat_out[turn] = jnp.concatenate([mean, spread], axis=0)

        def push(k, _):
            pltpu.make_async_remote_copy(
                src_ref=stat_out.at[turn],
                dst_ref=stat_in.at[turn, k - 1],
                send_sem=stat_send.at[turn],
                recv_sem=stat_recv.at[turn],
                device_id=device(k),
                device_id_type=MESH,
            ).start()
            return 0

        lax.fori_loop(1, count, push, 0)
        if turn < 2:
            rim_out[turn] = centred.astype(jnp.bfloat16).reshape(rows, depth, length, channels)
            for s in range(len(SIDES)):
                @pl.when(present(SIDES[s]))
                def _():
                    rim_copy(turn, s).start()
        return mean, spread

    def leaky(value):
        return jnp.where(value >= 0.0, value, 0.01 * value)

    def finish(turn, mean, spread):
        stat_all(turn).wait_recv()
        others = stat_in[turn]
        centre = (jnp.sum(others[:, 0:1, :], axis=0) + mean) / count
        offsets = others[:, 0:1, :] - centre
        total = jnp.sum(others[:, 1:2, :] + cells * (offsets * offsets), axis=0)
        total = total + spread + cells * ((mean - centre) * (mean - centre))
        scale = gain_ref[turn:turn + 1] * lax.rsqrt(total / (cells * count) + 1e-5)
        return centre, scale, shift_ref[turn:turn + 1], others

    def normalized_field(turn, value, mean, spread):
        centre, scale, shift, others = finish(turn, mean, spread)
        own = leaky((value - centre) * scale + shift).astype(jnp.bfloat16)
        field[1:rows + 1, 1:depth + 1] = own.reshape(rows, depth, length, channels)
        for s, (dy, dz) in enumerate(SIDES):
            ok = present((dy, dz))

            @pl.when(ok)
            def _():
                rim_arrival(turn, s).wait_recv()
                origin = (-(dy * nz + dz)) % count
                bias = others[origin - 1, 0:1, :] - centre
                raw = rim_in[turn, outer(dy, rows), outer(dz, depth)].astype(jnp.float32)
                field[outer(dy, rows), outer(dz, depth)] = leaky(
                    (raw + bias) * scale + shift
                ).astype(jnp.bfloat16)

            @pl.when(jnp.logical_not(ok))
            def _():
                slot = field.at[outer(dy, rows), outer(dz, depth)]
                slot[...] = jnp.zeros(slot.shape, jnp.bfloat16)

    def convolve(weight):
        left = jnp.concatenate(
            [
                field[p:p + rows, q:q + depth].reshape(cells, channels)
                for p in range(3) for q in range(3)
            ],
            axis=1,
        )
        parts = []
        for r in range(3):
            right = jnp.concatenate(
                [
                    weight[p, q, :, r * channels:(r + 1) * channels]
                    for p in range(3) for q in range(3)
                ],
                axis=1,
            )
            parts.append(
                lax.dot_general(
                    left, right, (((1,), (1,)), ((), ())), preferred_element_type=jnp.float32
                )
            )
        place = lax.rem(lax.broadcasted_iota(jnp.int32, (cells, channels), 0), length)
        before = jnp.where(place == 0, 0.0, pltpu.roll(parts[0], 1, 0))
        after = jnp.where(place == length - 1, 0.0, pltpu.roll(parts[2], cells - 1, 0))
        return parts[1] + before + after

    value = coarse_ref[...].reshape(cells, channels)
    for turn, weight in enumerate((one_ref, two_ref)):
        mean, spread = send(turn, value)
        normalized_field(turn, value, mean, spread)
        loads[turn].wait()
        value = convolve(weight)
    mean, spread = send(2, value)
    centre, scale, shift, _ = finish(2, mean, spread)
    out = leaky((value - centre) * scale + shift).astype(jnp.bfloat16)
    out_ref[...] = out.reshape(rows, depth, length, channels)

    for turn in range(3):
        stat_all(turn).wait_send()
        if turn < 2:
            for s in range(len(SIDES)):
                @pl.when(present(SIDES[s]))
                def _():
                    rim_copy(turn, s).wait_send()


def on_device(ny, nz, volume, down_weight, conv_one, conv_two, norm_gain, norm_shift):
    coarse = strided(volume, down_weight)
    rows, depth, length, channels = coarse.shape
    vmem = pl.BlockSpec(memory_space=pltpu.VMEM)
    hbm = pl.BlockSpec(memory_space=pl.ANY)
    count = ny * nz
    out = pl.pallas_call(
        functools.partial(kernel, ny, nz),
        out_shape=jax.ShapeDtypeStruct(coarse.shape, jnp.bfloat16),
        in_specs=[vmem, hbm, hbm, vmem, vmem],
        out_specs=vmem,
        scratch_shapes=[
            pltpu.VMEM(conv_one.shape, jnp.bfloat16),
            pltpu.VMEM(conv_two.shape, jnp.bfloat16),
            pltpu.VMEM((3, 2, channels), jnp.float32),
            pltpu.VMEM((3, count - 1, 2, channels), jnp.float32),
            pltpu.VMEM((2, rows, depth, length, channels), jnp.bfloat16),
            pltpu.VMEM((2, rows + 2, depth + 2, length, channels), jnp.bfloat16),
            pltpu.VMEM((rows + 2, depth + 2, length, channels), jnp.bfloat16),
            pltpu.SemaphoreType.DMA((2,)),
            pltpu.SemaphoreType.DMA((3,)),
            pltpu.SemaphoreType.DMA((3,)),
            pltpu.SemaphoreType.DMA((2, len(SIDES))),
            pltpu.SemaphoreType.DMA((2, len(SIDES))),
        ],
        compiler_params=pltpu.CompilerParams(
            collective_id=0, has_side_effects=True, vmem_limit_bytes=40 * 1024 * 1024
        ),
    )(coarse, conv_one, conv_two, norm_gain, norm_shift)
    return jnp.transpose(out, (3, 0, 1, 2))


def solution(mesh):
    return jax.shard_map(
        functools.partial(on_device, mesh.shape["gy"], mesh.shape["gz"]),
        mesh=mesh,
        in_specs=(P(None, "gy", "gz", None), P(), P(), P(), P(), P()),
        out_specs=P(None, "gy", "gz", None),
        check_vma=False,
    )
```

```python
import functools

import jax
import jax.numpy as jnp
from jax import lax
from jax.experimental import pallas as pl
from jax.experimental.pallas import tpu as pltpu
from jax.sharding import PartitionSpec as P

MESH = pl.DeviceIdType.MESH
SIDES = [(dy, dz) for dy in (-1, 0, 1) for dz in (-1, 0, 1) if (dy, dz) != (0, 0)]


def kernel(
    ny, nz,
    volume_hbm, down_hbm, one_hbm, two_hbm, gain_ref, shift_ref, out_ref,
    volume_ref, down_ref, wide, taps, pairs, one_ref, two_ref, right, stat_out, stat_in, rim_out, rim_in, field,
    load_sem, stat_send, stat_recv, rim_send, rim_recv,
):
    count = ny * nz
    my, mz = lax.axis_index("gy"), lax.axis_index("gz")
    me = my * nz + mz
    rows, depth, length, channels = out_ref.shape
    inputs = volume_ref.shape[0]
    cells = rows * depth * length

    loads = [
        pltpu.make_async_copy(volume_hbm, volume_ref, load_sem.at[0]),
        pltpu.make_async_copy(down_hbm, down_ref, load_sem.at[1]),
        pltpu.make_async_copy(one_hbm, one_ref, load_sem.at[2]),
        pltpu.make_async_copy(two_hbm, two_ref, load_sem.at[3]),
    ]
    for load in loads:
        load.start()

    def device(dy, dz):
        y, z = my + dy, mz + dz
        return (jnp.where(y >= ny, y - ny, y), jnp.where(z >= nz, z - nz, z))
    def peers(act):
        for dz in range(1, nz):
            act(0, dz)
        def body(dy, _):
            for dz in range(nz):
                act(dy, dz)
            return 0
        lax.fori_loop(1, ny, body, 0, unroll=True)

    barrier = pltpu.get_barrier_semaphore()

    def greet(dy, dz):
        pl.semaphore_signal(barrier, inc=1, device_id=device(dy, dz), device_id_type=MESH)

    peers(greet)

    def present(side):
        y, z = my + side[0], mz + side[1]
        return (y >= 0) & (y < ny) & (z >= 0) & (z < nz)

    def outer(d, n):
        return {-1: slice(0, 1), 0: slice(1, n + 1), 1: slice(n + 1, n + 2)}[d]

    def inner(d, n):
        return {-1: slice(0, 1), 0: slice(0, n), 1: slice(n - 1, n)}[d]

    def rim_copy(turn, s):
        dy, dz = SIDES[s]
        opposite = len(SIDES) - 1 - s
        return pltpu.make_async_remote_copy(
            src_ref=rim_out.at[turn, inner(dy, rows), inner(dz, depth)],
            dst_ref=rim_in.at[turn, outer(-dy, rows), outer(-dz, depth)],
            send_sem=rim_send.at[turn, s],
            recv_sem=rim_recv.at[turn, opposite],
            device_id=(my + dy, mz + dz),
            device_id_type=MESH,
        )

    def rim_arrival(turn, s):
        dy, dz = SIDES[s]
        slot = rim_in.at[turn, outer(dy, rows), outer(dz, depth)]
        return pltpu.make_async_remote_copy(
            src_ref=slot, dst_ref=slot,
            send_sem=rim_send.at[turn, s], recv_sem=rim_recv.at[turn, s],
            device_id=(my, mz), device_id_type=MESH,
        )

    def stat_all(turn):
        block = stat_in.at[turn, pl.ds(0, count - 1)]
        return pltpu.make_async_remote_copy(
            src_ref=block, dst_ref=block,
            send_sem=stat_send.at[turn], recv_sem=stat_recv.at[turn],
            device_id=(my, mz), device_id_type=MESH,
        )

    def send(turn, value):
        mean = jnp.sum(value, axis=0, keepdims=True) / cells
        centred = value - mean
        spread = jnp.sum(centred * centred, axis=0, keepdims=True)
        stat_out[turn] = jnp.concatenate([mean, spread], axis=0)

        def push(dy, dz):
            pltpu.make_async_remote_copy(
                src_ref=stat_out.at[turn],
                dst_ref=stat_in.at[turn, dy * nz + dz - 1],
                send_sem=stat_send.at[turn],
                recv_sem=stat_recv.at[turn],
                device_id=device(dy, dz),
                device_id_type=MESH,
            ).start()

        peers(push)
        if turn < 2:
            rim_out[turn] = centred.astype(jnp.bfloat16).reshape(rows, depth, length, channels)
            for s in range(len(SIDES)):
                @pl.when(present(SIDES[s]))
                def _():
                    rim_copy(turn, s).start()
        return mean, spread

    def leaky(value):
        return jnp.where(value >= 0.0, value, 0.01 * value)

    def finish(turn, mean, spread):
        stat_all(turn).wait_recv()
        others = stat_in[turn]
        centre = (jnp.sum(others[:, 0:1, :], axis=0) + mean) / count
        offsets = others[:, 0:1, :] - centre
        total = jnp.sum(others[:, 1:2, :] + cells * (offsets * offsets), axis=0)
        total = total + spread + cells * ((mean - centre) * (mean - centre))
        scale = gain_ref[turn:turn + 1] * lax.rsqrt(total / (cells * count) + 1e-5)
        return centre, scale, shift_ref[turn:turn + 1], others

    def normalized_field(turn, value, mean, spread):
        centre, scale, shift, others = finish(turn, mean, spread)
        own = leaky((value - centre) * scale + shift).astype(jnp.bfloat16)
        field[1:rows + 1, 1:depth + 1] = own.reshape(rows, depth, length, channels)
        for s, (dy, dz) in enumerate(SIDES):
            ok = present((dy, dz))

            @pl.when(ok)
            def _():
                rim_arrival(turn, s).wait_recv()
                origin = (-dy % ny) * nz + (-dz % nz)
                bias = others[origin - 1, 0:1, :] - centre
                raw = rim_in[turn, outer(dy, rows), outer(dz, depth)].astype(jnp.float32)
                field[outer(dy, rows), outer(dz, depth)] = leaky(
                    (raw + bias) * scale + shift
                ).astype(jnp.bfloat16)

            @pl.when(jnp.logical_not(ok))
            def _():
                slot = field.at[outer(dy, rows), outer(dz, depth)]
                slot[...] = jnp.zeros(slot.shape, jnp.bfloat16)

    def strided():
        loads[1].wait()
        taps[...] = down_ref[...].astype(jnp.float32)
        factor = jnp.concatenate(
            [
                jnp.concatenate(
                    [taps[pl.ds(4 * a + 2 * b + c, inputs, stride=8)] for a in range(2) for b in range(2)],
                    axis=0,
                )
                for c in range(2)
            ],
            axis=1,
        ).astype(jnp.bfloat16)
        loads[0].wait()
        wide[...] = volume_ref[...].astype(jnp.float32)
        made = []
        for y in range(rows):
            for z in range(depth):
                block = jnp.concatenate(
                    [wide[:, 2 * y + a, 2 * z + b] for a in range(2) for b in range(2)], axis=0
                ).astype(jnp.bfloat16)
                both = lax.dot_general(
                    block, factor, (((0,), (0,)), ((), ())), preferred_element_type=jnp.float32
                )
                start = (y * depth + z) * 2 * length
                made.append(0.0)
                for c in range(2):
                    pairs[c, start:start + 2 * length] = both[:, c * channels:(c + 1) * channels]
                    made[-1] += pairs[c, pl.ds(start + c, length, stride=2)]
        return jnp.concatenate(made, axis=0)

    def arrange(weight):
        right[...] = jnp.concatenate(
            [
                jnp.concatenate(
                    [weight[p, q, :, r * channels:(r + 1) * channels].T for r in range(3)], axis=1
                )
                for p in range(3) for q in range(3)
            ],
            axis=0,
        )

    def convolve():
        left = jnp.concatenate(
            [
                field[p:p + rows, q:q + depth].reshape(cells, channels)
                for p in range(3) for q in range(3)
            ],
            axis=1,
        )
        product = jnp.dot(left, right[...], preferred_element_type=jnp.float32)
        parts = [product[:, r * channels:(r + 1) * channels] for r in range(3)]
        place = lax.rem(lax.broadcasted_iota(jnp.int32, (cells, channels), 0), length)
        before = jnp.where(place == 0, 0.0, pltpu.roll(parts[0], 1, 0))
        after = jnp.where(place == length - 1, 0.0, pltpu.roll(parts[2], cells - 1, 0))
        return parts[1] + before + after

    value = strided()
    pl.semaphore_wait(barrier, count - 1)
    for turn, weight in enumerate((one_ref, two_ref)):
        mean, spread = send(turn, value)
        loads[2 + turn].wait()
        arrange(weight)
        normalized_field(turn, value, mean, spread)
        value = convolve()
    mean, spread = send(2, value)
    centre, scale, shift, _ = finish(2, mean, spread)
    out = leaky((value - centre) * scale + shift).astype(jnp.bfloat16)
    out_ref[...] = out.reshape(rows, depth, length, channels)

    for turn in range(3):
        stat_all(turn).wait_send()
        if turn < 2:
            for s in range(len(SIDES)):
                @pl.when(present(SIDES[s]))
                def _():
                    rim_copy(turn, s).wait_send()


def on_device(ny, nz, volume, down_weight, conv_one, conv_two, norm_gain, norm_shift):
    inputs, rows, depth, length = volume.shape
    rows, depth, length = rows // 2, depth // 2, length // 2
    channels = down_weight.shape[0]
    cells = rows * depth * length
    down = jnp.transpose(down_weight, (1, 2, 3, 4, 0)).reshape(8 * inputs, channels)
    vmem = pl.BlockSpec(memory_space=pltpu.VMEM)
    hbm = pl.BlockSpec(memory_space=pltpu.HBM)
    count = ny * nz
    out = pl.pallas_call(
        functools.partial(kernel, ny, nz),
        out_shape=jax.ShapeDtypeStruct((rows, depth, length, channels), jnp.bfloat16),
        in_specs=[hbm, hbm, hbm, hbm, vmem, vmem],
        out_specs=vmem,
        scratch_shapes=[
            pltpu.VMEM(volume.shape, jnp.bfloat16),
            pltpu.VMEM(down.shape, jnp.bfloat16),
            pltpu.VMEM(volume.shape, jnp.float32),
            pltpu.VMEM(down.shape, jnp.float32),
            pltpu.VMEM((2, 2 * cells, channels), jnp.float32),
            pltpu.VMEM(conv_one.shape, jnp.bfloat16),
            pltpu.VMEM(conv_two.shape, jnp.bfloat16),
            pltpu.VMEM((9 * channels, 3 * channels), jnp.bfloat16),
            pltpu.VMEM((3, 2, channels), jnp.float32),
            pltpu.VMEM((3, count - 1, 2, channels), jnp.float32),
            pltpu.VMEM((2, rows, depth, length, channels), jnp.bfloat16),
            pltpu.VMEM((2, rows + 2, depth + 2, length, channels), jnp.bfloat16),
            pltpu.VMEM((rows + 2, depth + 2, length, channels), jnp.bfloat16),
            pltpu.SemaphoreType.DMA((4,)),
            pltpu.SemaphoreType.DMA((3,)),
            pltpu.SemaphoreType.DMA((3,)),
            pltpu.SemaphoreType.DMA((2, len(SIDES))),
            pltpu.SemaphoreType.DMA((2, len(SIDES))),
        ],
        compiler_params=pltpu.CompilerParams(
            collective_id=0, has_side_effects=True, vmem_limit_bytes=56 * 1024 * 1024
        ),
    )(volume, down, conv_one, conv_two, norm_gain, norm_shift)
    return jnp.transpose(out, (3, 0, 1, 2))


def solution(mesh):
    return jax.shard_map(
        functools.partial(on_device, mesh.shape["gy"], mesh.shape["gz"]),
        mesh=mesh,
        in_specs=(P(None, "gy", "gz", None), P(), P(), P(), P(), P()),
        out_specs=P(None, "gy", "gz", None),
        check_vma=False,
    )
```
